1024 devices in a mesh: vir: 64 (over y, x), occ: 8 (over z), rep: 2 (over core).
Axes of the slice: x: 8, y: 8, z: 8, core: 2. Of those that a mesh axis runs over, the one named last changes fastest.
Arguments:
- amplitudes: bfloat16 [64, 8, 64, 128, 128], P('vir', 'occ', None, 'rep'), may hold values from -6 to 6
- cycle_ints: bfloat16 [8, 1, 64, 128, 128], P('occ'), may hold values from -0.125 to 0.125
- cycle_src: int32 [64, 2], replicated, may hold values from 0 to 63
- cycle_wsel: int32 [64, 2], replicated, may hold values from 0 to 63
- ladder_src: int32 [64, 2], replicated, may hold values from 0 to 63
- owner_order: int32 [64], replicated, may hold values from 0 to 63, each once
- first_integral_blocks: bfloat16 [6, 64, 2, 128, 128], P(None, 'vir'), may hold values from -0.15625 to 0.15625
- right_ints: bfloat16 [6, 64, 2, 128, 128], P(None, 'vir'), may hold values from -0.5 to 0.5
Outputs:
- cycle_part: bfloat16 [64, 1, 64, 128, 128], P('vir', None, 'occ', 'rep')
- ladder_part: bfloat16 [64, 8, 64, 128, 128], P(None, 'occ', 'vir', 'rep')
The draws below stay inside these ranges and needn't reach their ends.
All inputs are finite; a program needn't handle non-finite values.
Results may differ from the reference program's by a relative error of at most 0.0049.
Values may be sent and summed in bfloat16 or wider, within the bound.
No kernel may reach another device: no remote copies, remote signals or barrier semaphores. Data moves between devices by JAX's collectives and lax.ppermute only.
A program may use at most 64 MiB of HBM per device.

```python
import jax
import jax.numpy as jnp
from jax import lax

TILE = 128
NQ = 6
LTERMS = 2
RTERMS = 2
NJ = 1
NI = 64
NK = 8
NNZ = 64
NW = 64


def place_ends(entries, key, low, high):
    longest = entries.shape.index(max(entries.shape))
    spots = []
    for shift in (0, 1):
        where = [jax.random.randint(jax.random.fold_in(key, axis), (), 0, length) for axis, length in enumerate(entries.shape)]
        where[longest] = (where[longest] + shift) % entries.shape[longest]
        spots.append(tuple(where))
    return entries.at[spots[0]].set(low).at[spots[1]].set(high)


def shard_levels(own_key, extent, shards, least, top_value):
    def one(dim, parts):
        steps = jax.random.uniform(jax.random.fold_in(jax.random.fold_in(own_key, 6), dim), (parts,), jnp.float32, least / len(shards), top_value / len(shards))
        return jnp.repeat(jnp.exp(steps), extent[dim] // parts).reshape((-1,) + (1,) * (len(extent) - dim - 1))

    factor_of = one(*shards[0])
    for cut in shards[1:]:
        factor_of = factor_of * one(*cut)
    return factor_of


def noise(rng, dims, scale, limit, cuts=(), kind=jnp.bfloat16):
    array = scale * jax.random.normal(rng, dims, jnp.float32)
    if cuts:
        array = array * shard_levels(rng, dims, cuts, -0.22, 0.18)
    return jnp.clip(array, -limit, limit).astype(kind)


def setup_inputs(seed: int = 0) -> dict:
    keys = jax.random.split(jax.random.key(seed), 9)
    amplitudes = noise(keys[0], (NI, NK, NNZ, TILE, TILE), 1.0, 6.0, ((0, 64), (1, 8), (3, 2)))
    cycle_ints = noise(keys[1], (NK, NJ, NW, TILE, TILE), (RTERMS * TILE * NK) ** -0.5, 0.125, ((0, 8),))
    cycle_src = place_ends(jax.random.randint(keys[2], (NNZ, RTERMS), 0, NNZ), jax.random.fold_in(keys[2], 1), 0, NNZ - 1).astype(jnp.int32)
    cycle_wsel = place_ends(jax.random.randint(keys[3], (NNZ, RTERMS), 0, NW), jax.random.fold_in(keys[3], 1), 0, NW - 1).astype(jnp.int32)
    ladder_src = place_ends(jax.random.randint(keys[4], (NNZ, LTERMS), 0, NNZ), jax.random.fold_in(keys[4], 1), 0, NNZ - 1).astype(jnp.int32)
    owner_order = jax.random.permutation(keys[5], NNZ).astype(jnp.int32)
    first_integral_blocks = noise(keys[6], (NQ, NNZ, LTERMS, TILE, TILE), (NQ * LTERMS * TILE) ** -0.5, 0.15625, ((1, 64),))
    right_ints = noise(keys[7], (NQ, NNZ, LTERMS, TILE, TILE), TILE ** -0.5, 0.5, ((1, 64),))
    return dict(amplitudes=amplitudes, cycle_ints=cycle_ints, cycle_src=cycle_src, cycle_wsel=cycle_wsel, ladder_src=ladder_src, owner_order=owner_order, first_integral_blocks=first_integral_blocks, right_ints=right_ints)


def reference(amplitudes, cycle_ints, cycle_src, cycle_wsel, ladder_src, owner_order, first_integral_blocks, right_ints):
    def cycle_one(slot_index):
        amp_tiles = jnp.take(amplitudes, cycle_src[slot_index], axis=2).astype(jnp.float32)
        int_tiles = jnp.take(cycle_ints, cycle_wsel[slot_index], axis=2).astype(jnp.float32)
        return jnp.einsum("ikpac,kjpcb->ijab", amp_tiles, int_tiles).astype(jnp.bfloat16)

    cycle_stack = lax.map(cycle_one, jnp.arange(NNZ, dtype=jnp.int32))
    cycle_part = jnp.transpose(cycle_stack, (1, 2, 0, 3, 4))

    def ladder_one(position):
        slot_ids = ladder_src[owner_order[position]]
        amp_tiles = jnp.take(amplitudes, slot_ids, axis=2).astype(jnp.float32)
        first_virtual_tiles = jnp.take(first_integral_blocks, position, axis=1).astype(jnp.float32)
        right_tiles = jnp.take(right_ints, position, axis=1).astype(jnp.float32)

        def add_vector(summed, pieces):
            first_vector_slot, right_q = pieces
            halved_contribution = jnp.einsum("ikpec,pdc->ikped", amp_tiles, right_q)
            halved_contribution = lax.optimization_barrier(halved_contribution.astype(jnp.bfloat16)).astype(jnp.float32)
            return summed + jnp.einsum("pae,ikped->ikad", first_vector_slot, halved_contribution), None

        initial = jnp.zeros((NI, NK, TILE, TILE), jnp.float32)
        summed, discarded_value = lax.scan(add_vector, initial, (first_virtual_tiles, right_tiles))
        return summed.astype(jnp.bfloat16)

    ladder_stack = lax.map(ladder_one, jnp.arange(NNZ, dtype=jnp.int32))
    ladder_part = jnp.transpose(ladder_stack, (1, 2, 0, 3, 4))
    return cycle_part, ladder_part
```

```python
import jax
import jax.numpy as jnp
from jax import lax
from jax.experimental import pallas as pl
from jax.experimental.pallas import tpu as pltpu
from jax.sharding import PartitionSpec as P

GROUP = 16


def gather_kernel(order_ref, src_ref, tiles_ref, out_ref):
    count, terms = out_ref.shape[0], out_ref.shape[1]

    def one(m, carry):
        slot = order_ref[m]
        for p in range(terms):
            out_ref[m, p] = tiles_ref[src_ref[p, slot]]
        return carry

    lax.fori_loop(0, count, one, 0, unroll=8)


def whole(shape):
    return pl.BlockSpec(shape, lambda g, *_: (0,) * len(shape))


def gather_tiles(order, src, tiles):
    terms, count = src.shape
    out_shape = (count, terms) + tiles.shape[1:]
    return pl.pallas_call(
        gather_kernel,
        grid_spec=pltpu.PrefetchScalarGridSpec(
            num_scalar_prefetch=2,
            grid=(1,),
            in_specs=[whole(tiles.shape)],
            out_specs=whole(out_shape),
        ),
        out_shape=jax.ShapeDtypeStruct(out_shape, tiles.dtype),
        compiler_params=pltpu.CompilerParams(vmem_limit_bytes=8 << 20),
        cost_estimate=pl.CostEstimate(flops=0, bytes_accessed=4 << 20, transcendentals=0),
        name="outgoing_tiles",
    )(order, src, tiles)


def cycle_kernel(me_ref, src_ref, wsel_ref, amps_ref, ints_ref, *out_refs):
    terms, holders, share = src_ref.shape[0], len(out_refs), out_refs[0].shape[0]
    me = me_ref[0]
    for step, out_ref in enumerate(out_refs):
        base = lax.rem(me + step, holders) * share

        def one(t, carry):
            s = base + t
            left = jnp.concatenate([amps_ref[src_ref[p, s]] for p in range(terms)], axis=1)
            right = jnp.concatenate([ints_ref[wsel_ref[p, s]] for p in range(terms)], axis=0)
            total = jnp.dot(left, right, preferred_element_type=jnp.float32)
            out_ref[t] = total.astype(out_ref.dtype)
            return carry

        lax.fori_loop(0, share, one, 0, unroll=4)


def cycle_partials(me, holders, src, wsel, amps, ints):
    share = src.shape[1] // holders
    out_shape = (share,) + amps.shape[1:]
    return pl.pallas_call(
        cycle_kernel,
        grid_spec=pltpu.PrefetchScalarGridSpec(
            num_scalar_prefetch=3,
            grid=(1,),
            in_specs=[whole(amps.shape), whole(ints.shape)],
            out_specs=[whole(out_shape)] * holders,
        ),
        out_shape=[jax.ShapeDtypeStruct(out_shape, jnp.bfloat16)] * holders,
        compiler_params=pltpu.CompilerParams(vmem_limit_bytes=12 << 20),
        cost_estimate=pl.CostEstimate(flops=2 * 64 * 64 * 256 * 128, bytes_accessed=4 << 20, transcendentals=0),
        name="cycle_partials",
    )(me, src, wsel, amps, ints)


def ladder_kernel(amps_ref, left_ref, right_ref, own_ref, other_ref):
    group, terms, rows, width = amps_ref.shape
    vectors = right_ref.shape[1] // width
    half = own_ref.shape[1]
    left = left_ref[...]
    sub = 4
    for start in range(0, group, sub):
        halves = []
        for p in range(terms):
            tiles = amps_ref[start : start + sub, p].reshape(sub * rows, width)
            product = lax.dot_general(
                tiles, right_ref[p], (((1,), (1,)), ((), ())), preferred_element_type=jnp.float32
            )
            halves.append(product.astype(jnp.bfloat16))
        for first in range(0, sub, 2):
            columns = []
            for i in (first, first + 1):
                columns.append(
                    jnp.concatenate(
                        [
                            halves[p][i * rows : (i + 1) * rows, q * width : (q + 1) * width]
                            for p in range(terms)
                            for q in range(vectors)
                        ],
                        axis=0,
                    )
                )
            summed = jnp.dot(left, jnp.concatenate(columns, axis=1), preferred_element_type=jnp.float32)
            for place in range(2):
                tile = summed[:, place * width : (place + 1) * width]
                own_ref[start + first + place] = tile[:half]
                other_ref[start + first + place] = tile[half:].astype(other_ref.dtype)


def ladder_partials(amps, left, right):
    items, terms, rows, width = amps.shape
    half = left.shape[0] // 2
    return pl.pallas_call(
        ladder_kernel,
        grid=(items // GROUP,),
        in_specs=[
            pl.BlockSpec((GROUP, terms, rows, width), lambda g: (g, 0, 0, 0)),
            pl.BlockSpec(left.shape, lambda g: (0, 0)),
            pl.BlockSpec(right.shape, lambda g: (0, 0, 0)),
        ],
        out_specs=[
            pl.BlockSpec((GROUP, half, width), lambda g: (g, 0, 0)),
            pl.BlockSpec((GROUP, half, width), lambda g: (g, 0, 0)),
        ],
        out_shape=[
            jax.ShapeDtypeStruct((items, half, width), jnp.float32),
            jax.ShapeDtypeStruct((items, half, width), jnp.bfloat16),
        ],
        compiler_params=pltpu.CompilerParams(vmem_limit_bytes=12 << 20),
        cost_estimate=pl.CostEstimate(flops=32 << 27, bytes_accessed=6 << 20, transcendentals=0),
        name="ladder_partials",
    )(amps, left, right)


def sum_kernel(*refs):
    out_ref = refs[-1]
    total = refs[0][...].astype(jnp.float32)
    for part_ref in refs[1:-1]:
        total = total + part_ref[...].astype(jnp.float32)
    out_ref[...] = total.astype(out_ref.dtype)


def sum_parts(parts):
    size = parts[0].size
    return pl.pallas_call(
        sum_kernel,
        in_specs=[pl.BlockSpec(memory_space=pltpu.VMEM)] * len(parts),
        out_specs=pl.BlockSpec(memory_space=pltpu.VMEM),
        out_shape=jax.ShapeDtypeStruct(parts[0].shape, parts[0].dtype),
        cost_estimate=pl.CostEstimate(flops=8 * size, bytes_accessed=18 * size, transcendentals=0),
        name="sum_parts",
    )(*parts)


def shards(
    amplitudes,
    cycle_ints,
    cycle_src,
    cycle_wsel,
    ladder_src,
    owner_order,
    first_integral_blocks,
    right_ints,
):
    held_tiles = amplitudes[0, 0]
    tile_count, row_count, width = held_tiles.shape

    outgoing = gather_tiles(owner_order, ladder_src.T, held_tiles)
    arriving = lax.all_to_all(outgoing, "vir", split_axis=0, concat_axis=0, tiled=True)

    holders = lax.axis_size("occ")
    me = lax.axis_index("occ").astype(jnp.int32).reshape(1)
    partials = cycle_partials(me, holders, cycle_src.T, cycle_wsel.T, held_tiles, cycle_ints[0, 0])
    parts = [partials[0]]
    for step in sorted(range(1, holders), key=lambda step: (abs(step - holders // 2), step)):
        ring = [(k, (k + step) % holders) for k in range(holders)]
        parts.append(lax.ppermute(partials[step], "occ", ring))
    cycle_part = sum_parts(parts)
    arriving, cycle_part = lax.optimization_barrier((arriving, cycle_part))
    cycle_part = cycle_part[None, None]

    replica = lax.axis_index("rep")
    left = lax.dynamic_slice_in_dim(first_integral_blocks[:, 0], replica * row_count, row_count, 3)
    left = jnp.transpose(left, (2, 1, 0, 3)).reshape(width, -1)
    own_rows = lax.dynamic_slice_in_dim(left, replica * row_count, row_count, 0)
    other_rows = lax.dynamic_slice_in_dim(left, (1 - replica) * row_count, row_count, 0)
    left = jnp.concatenate([own_rows, other_rows], axis=0)
    right = jnp.transpose(right_ints[:, 0], (1, 0, 2, 3)).reshape(right_ints.shape[2], -1, width)

    own, other = ladder_partials(arriving, left, right)
    received = lax.ppermute(other, "rep", [(0, 1), (1, 0)])
    ladder_part = (own + received.astype(jnp.float32)).astype(jnp.bfloat16)[:, None, None]
    return (cycle_part, ladder_part)


def solution(mesh):
    in_specs = (
        P("vir", "occ", None, "rep", None),
        P("occ", None, None, None, None),
        P(),
        P(),
        P(),
        P(),
        P(None, "vir", None, None, None),
        P(None, "vir", None, None, None),
    )
    out_specs = (P("vir", None, "occ", "rep", None), P(None, "occ", "vir", "rep", None))
    return jax.shard_map(shards, mesh=mesh, in_specs=in_specs, out_specs=out_specs, check_vma=False)
```

```python
import jax
import jax.numpy as jnp
from jax import lax
from jax.experimental import pallas as pl
from jax.experimental.pallas import tpu as pltpu
from jax.sharding import PartitionSpec as P

GROUP = 16
TOGETHER = 8
SENDS = (4, 3, 5, 2, 6, 1, 7)
SPLITS = 4


def gather_kernel(order_hbm, src_hbm, tiles_hbm, out_hbm, order_ref, src_ref, tiles_ref, out_ref, sems):
    count, terms = out_ref.shape[0], out_ref.shape[1]
    loads = [
        pltpu.make_async_copy(order_hbm, order_ref, sems.at[0]),
        pltpu.make_async_copy(src_hbm, src_ref, sems.at[1]),
        pltpu.make_async_copy(tiles_hbm, tiles_ref, sems.at[2]),
    ]
    for load in loads:
        load.start()
    for load in loads:
        load.wait()

    def one(m, carry):
        slot = order_ref[m]
        for p in range(terms):
            out_ref[m, p] = tiles_ref[src_ref[p, slot]]
        return carry

    share = count // SPLITS
    stores = []
    for part in range(SPLITS):
        lax.fori_loop(part * share, (part + 1) * share, one, 0, unroll=8)
        block = pl.ds(part * share, share)
        stores.append(pltpu.make_async_copy(out_ref.at[block], out_hbm.at[block], sems.at[3 + part]))
        stores[-1].start()
    for store in stores:
        store.wait()


def whole(shape):
    return pl.BlockSpec(shape, lambda g, *_: (0,) * len(shape))


def gather_tiles(order, src, tiles):
    terms, count = src.shape
    out_shape = (count, terms) + tiles.shape[1:]
    return pl.pallas_call(
        gather_kernel,
        in_specs=[pl.BlockSpec(memory_space=pltpu.HBM)] * 3,
        out_specs=pl.BlockSpec(memory_space=pltpu.HBM),
        out_shape=jax.ShapeDtypeStruct(out_shape, tiles.dtype),
        scratch_shapes=[
            pltpu.SMEM(order.shape, order.dtype),
            pltpu.SMEM(src.shape, src.dtype),
            pltpu.VMEM(tiles.shape, tiles.dtype),
            pltpu.VMEM(out_shape, tiles.dtype),
            pltpu.SemaphoreType.DMA((3 + SPLITS,)),
        ],
        compiler_params=pltpu.CompilerParams(vmem_limit_bytes=8 << 20),
        cost_estimate=pl.CostEstimate(flops=0, bytes_accessed=4 << 20, transcendentals=0),
        name="outgoing_tiles",
    )(order, src, tiles)


def cycle_kernel(me_ref, src_ref, wsel_ref, amps_ref, ints_ref, *refs):
    *out_hbm, out_ref, sems = refs
    terms, holders, share = src_ref.shape[0], out_ref.shape[0], out_ref.shape[1]
    me = me_ref[0]
    stores = []
    for step in SENDS + (0,):
        base = lax.rem(me + step, holders) * share

        def one(t, carry):
            s = base + t
            left = jnp.concatenate([amps_ref[src_ref[p, s]] for p in range(terms)], axis=1)
            right = jnp.concatenate([ints_ref[wsel_ref[p, s]] for p in range(terms)], axis=0)
            total = jnp.dot(left, right, preferred_element_type=jnp.float32)
            out_ref[step, t] = total.astype(out_ref.dtype)
            return carry

        lax.fori_loop(0, share, one, 0, unroll=4)
        stores.append(pltpu.make_async_copy(out_ref.at[step], out_hbm[step], sems.at[step]))
        stores[-1].start()
    for store in stores:
        store.wait()


def cycle_partials(me, holders, src, wsel, amps, ints):
    share = src.shape[1] // holders
    out_shape = (share,) + amps.shape[1:]
    return pl.pallas_call(
        cycle_kernel,
        grid_spec=pltpu.PrefetchScalarGridSpec(
            num_scalar_prefetch=3,
            grid=(1,),
            in_specs=[whole(amps.shape), whole(ints.shape)],
            out_specs=[pl.BlockSpec(memory_space=pltpu.HBM)] * holders,
            scratch_shapes=[
                pltpu.VMEM((holders,) + out_shape, jnp.bfloat16),
                pltpu.SemaphoreType.DMA((holders,)),
            ],
        ),
        out_shape=[jax.ShapeDtypeStruct(out_shape, jnp.bfloat16)] * holders,
        compiler_params=pltpu.CompilerParams(vmem_limit_bytes=12 << 20),
        cost_estimate=pl.CostEstimate(flops=2 * 64 * 64 * 256 * 128, bytes_accessed=4 << 20, transcendentals=0),
        name="cycle_partials",
    )(me, src, wsel, amps, ints)


def ladder_kernel(amps_ref, left_ref, right_ref, own_ref, other_ref):
    group, terms, rows, width = amps_ref.shape
    vectors = right_ref.shape[1] // width
    half = own_ref.shape[1]
    left = left_ref[...]
    sub = min(TOGETHER, group)
    for start in range(0, group, sub):
        halves = []
        for p in range(terms):
            tiles = amps_ref[start : start + sub, p].reshape(sub * rows, width)
            product = lax.dot_general(
                tiles, right_ref[p], (((1,), (1,)), ((), ())), preferred_element_type=jnp.float32
            )
            halves.append(product.astype(jnp.bfloat16))
        for first in range(0, sub, 2):
            columns = []
            for i in (first, first + 1):
                columns.append(
                    jnp.concatenate(
                        [
                            halves[p][i * rows : (i + 1) * rows, q * width : (q + 1) * width]
                            for p in range(terms)
                            for q in range(vectors)
                        ],
                        axis=0,
                    )
                )
            summed = jnp.dot(left, jnp.concatenate(columns, axis=1), preferred_element_type=jnp.float32)
            for place in range(2):
                tile = summed[:, place * width : (place + 1) * width]
                own_ref[start + first + place] = tile[:half]
                other_ref[start + first + place] = tile[half:].astype(other_ref.dtype)


def ladder_partials(amps, left, right):
    items, terms, rows, width = amps.shape
    half = left.shape[0] // 2
    return pl.pallas_call(
        ladder_kernel,
        grid=(items // GROUP,),
        in_specs=[
            pl.BlockSpec((GROUP, terms, rows, width), lambda g: (g, 0, 0, 0)),
            pl.BlockSpec(left.shape, lambda g: (0, 0)),
            pl.BlockSpec(right.shape, lambda g: (0, 0, 0)),
        ],
        out_specs=[
            pl.BlockSpec((GROUP, half, width), lambda g: (g, 0, 0)),
            pl.BlockSpec((GROUP, half, width), lambda g: (g, 0, 0)),
        ],
        out_shape=[
            jax.ShapeDtypeStruct((items, half, width), jnp.float32),
            jax.ShapeDtypeStruct((items, half, width), jnp.bfloat16),
        ],
        compiler_params=pltpu.CompilerParams(vmem_limit_bytes=12 << 20),
        cost_estimate=pl.CostEstimate(flops=32 << 27, bytes_accessed=6 << 20, transcendentals=0),
        name="ladder_partials",
    )(amps, left, right)


def sum_kernel(*refs):
    out_ref = refs[-1]
    total = refs[0][...].astype(jnp.float32)
    for part_ref in refs[1:-1]:
        total = total + part_ref[...].astype(jnp.float32)
    out_ref[...] = total.astype(out_ref.dtype)


def sum_parts(parts):
    size = parts[0].size
    return pl.pallas_call(
        sum_kernel,
        in_specs=[pl.BlockSpec(memory_space=pltpu.VMEM)] * len(parts),
        out_specs=pl.BlockSpec(memory_space=pltpu.VMEM),
        out_shape=jax.ShapeDtypeStruct(parts[0].shape, parts[0].dtype),
        cost_estimate=pl.CostEstimate(flops=8 * size, bytes_accessed=18 * size, transcendentals=0),
        name="sum_parts",
    )(*parts)


def shards(
    amplitudes,
    cycle_ints,
    cycle_src,
    cycle_wsel,
    ladder_src,
    owner_order,
    first_integral_blocks,
    right_ints,
):
    held_tiles = amplitudes[0, 0]
    tile_count, row_count, width = held_tiles.shape

    outgoing = gather_tiles(owner_order, ladder_src.T, held_tiles)
    arriving = lax.all_to_all(outgoing, "vir", split_axis=0, concat_axis=0, tiled=True)

    holders = lax.axis_size("occ")
    me = lax.axis_index("occ").astype(jnp.int32).reshape(1)
    partials = cycle_partials(me, holders, cycle_src.T, cycle_wsel.T, held_tiles, cycle_ints[0, 0])
    parts = [partials[0]]
    for step in SENDS:
        ring = [(k, (k + step) % holders) for k in range(holders)]
        parts.append(lax.ppermute(partials[step], "occ", ring))
    arriving, *parts = lax.optimization_barrier((arriving, *parts))
    cycle_part = sum_parts(parts)[None, None]

    replica = lax.axis_index("rep")
    left = lax.dynamic_slice_in_dim(first_integral_blocks[:, 0], replica * row_count, row_count, 3)
    left = jnp.transpose(left, (2, 1, 0, 3)).reshape(width, -1)
    own_rows = lax.dynamic_slice_in_dim(left, replica * row_count, row_count, 0)
    other_rows = lax.dynamic_slice_in_dim(left, (1 - replica) * row_count, row_count, 0)
    left = jnp.concatenate([own_rows, other_rows], axis=0)
    right = jnp.transpose(right_ints[:, 0], (1, 0, 2, 3)).reshape(right_ints.shape[2], -1, width)

    own, other = ladder_partials(arriving, left, right)
    received = lax.ppermute(other, "rep", [(0, 1), (1, 0)])
    ladder_part = (own + received.astype(jnp.float32)).astype(jnp.bfloat16)[:, None, None]
    return (cycle_part, ladder_part)


def solution(mesh):
    in_specs = (
        P("vir", "occ", None, "rep", None),
        P("occ", None, None, None, None),
        P(),
        P(),
        P(),
        P(),
        P(None, "vir", None, None, None),
        P(None, "vir", None, None, None),
    )
    out_specs = (P("vir", None, "occ", "rep", None), P(None, "occ", "vir", "rep", None))
    return jax.shard_map(shards, mesh=mesh, in_specs=in_specs, out_specs=out_specs, check_vma=False)
```

```python
import jax
import jax.numpy as jnp
from jax import lax
from jax.experimental import pallas as pl
from jax.experimental.pallas import tpu as pltpu
from jax.sharding import PartitionSpec as P

GROUP = 16
TOGETHER = 8
SENDS = (4, 3, 5, 2, 6, 1, 7)
SPLITS = 4


def gather_kernel(order_hbm, src_hbm, tiles_hbm, out_hbm, order_ref, src_ref, tiles_ref, out_ref, sems):
    count, terms = out_ref.shape[0], out_ref.shape[1]
    loads = [
        pltpu.make_async_copy(order_hbm, order_ref, sems.at[0]),
        pltpu.make_async_copy(src_hbm, src_ref, sems.at[1]),
        pltpu.make_async_copy(tiles_hbm, tiles_ref, sems.at[2]),
    ]
    for load in loads:
        load.start()
    for load in loads:
        load.wait()

    def one(m, carry):
        slot = order_ref[m]
        for p in range(terms):
            out_ref[m, p] = tiles_ref[src_ref[p, slot]]
        return carry

    share = count // SPLITS
    stores = []
    for part in range(SPLITS):
        lax.fori_loop(part * share, (part + 1) * share, one, 0, unroll=8)
        block = pl.ds(part * share, share)
        stores.append(pltpu.make_async_copy(out_ref.at[block], out_hbm.at[block], sems.at[3 + part]))
        stores[-1].start()
    for store in stores:
        store.wait()


def in_hbm(array):
    return pltpu.with_memory_space_constraint(array, pltpu.HBM)


def whole(shape):
    return pl.BlockSpec(shape, lambda g, *_: (0,) * len(shape))


def gather_tiles(order, src, tiles):
    terms, count = src.shape
    out_shape = (count, terms) + tiles.shape[1:]
    return pl.pallas_call(
        gather_kernel,
        in_specs=[pl.BlockSpec(memory_space=pltpu.HBM)] * 3,
        out_specs=pl.BlockSpec(memory_space=pltpu.HBM),
        out_shape=pltpu.HBM(out_shape, tiles.dtype),
        scratch_shapes=[
            pltpu.SMEM(order.shape, order.dtype),
            pltpu.SMEM(src.shape, src.dtype),
            pltpu.VMEM(tiles.shape, tiles.dtype),
            pltpu.VMEM(out_shape, tiles.dtype),
            pltpu.SemaphoreType.DMA((3 + SPLITS,)),
        ],
        compiler_params=pltpu.CompilerParams(vmem_limit_bytes=8 << 20),
        cost_estimate=pl.CostEstimate(flops=0, bytes_accessed=4 << 20, transcendentals=0),
        name="outgoing_tiles",
    )(in_hbm(order), in_hbm(src), in_hbm(tiles))


def cycle_kernel(me_ref, src_ref, wsel_ref, amps_ref, ints_ref, *refs):
    *out_hbm, out_ref, sems = refs
    terms, holders, share = src_ref.shape[0], out_ref.shape[0], out_ref.shape[1]
    me = me_ref[0]
    stores = []
    for step in SENDS + (0,):
        base = lax.rem(me + step, holders) * share

        def one(t, carry):
            s = base + t
            left = jnp.concatenate([amps_ref[src_ref[p, s]] for p in range(terms)], axis=1)
            right = jnp.concatenate([ints_ref[wsel_ref[p, s]] for p in range(terms)], axis=0)
            total = jnp.dot(left, right, preferred_element_type=jnp.float32)
            out_ref[step, t] = total.astype(out_ref.dtype)
            return carry

        lax.fori_loop(0, share, one, 0, unroll=4)
        stores.append(pltpu.make_async_copy(out_ref.at[step], out_hbm[step], sems.at[step]))
        stores[-1].start()
    for store in stores:
        store.wait()


def cycle_partials(me, holders, src, wsel, amps, ints):
    share = src.shape[1] // holders
    out_shape = (share,) + amps.shape[1:]
    return pl.pallas_call(
        cycle_kernel,
        grid_spec=pltpu.PrefetchScalarGridSpec(
            num_scalar_prefetch=3,
            grid=(1,),
            in_specs=[whole(amps.shape), whole(ints.shape)],
            out_specs=[pl.BlockSpec(memory_space=pltpu.HBM)] * holders,
            scratch_shapes=[
                pltpu.VMEM((holders,) + out_shape, jnp.bfloat16),
                pltpu.SemaphoreType.DMA((holders,)),
            ],
        ),
        out_shape=[pltpu.HBM(out_shape, jnp.bfloat16)] * holders,
        compiler_params=pltpu.CompilerParams(vmem_limit_bytes=12 << 20),
        cost_estimate=pl.CostEstimate(flops=2 * 64 * 64 * 256 * 128, bytes_accessed=4 << 20, transcendentals=0),
        name="cycle_partials",
    )(me, src, wsel, amps, ints)


def ladder_kernel(amps_ref, left_ref, right_ref, own_ref, other_ref):
    group, terms, rows, width = amps_ref.shape
    vectors = right_ref.shape[1] // width
    half = own_ref.shape[1]
    left = left_ref[...]
    sub = min(TOGETHER, group)
    for start in range(0, group, sub):
        halves = []
        for p in range(terms):
            tiles = amps_ref[start : start + sub, p].reshape(sub * rows, width)
            product = lax.dot_general(
                tiles, right_ref[p], (((1,), (1,)), ((), ())), preferred_element_type=jnp.float32
            )
            halves.append(product.astype(jnp.bfloat16))
        for first in range(0, sub, 2):
            columns = []
            for i in (first, first + 1):
                columns.append(
                    jnp.concatenate(
                        [
                            halves[p][i * rows : (i + 1) * rows, q * width : (q + 1) * width]
                            for p in range(terms)
                            for q in range(vectors)
                        ],
                        axis=0,
                    )
                )
            summed = jnp.dot(left, jnp.concatenate(columns, axis=1), preferred_element_type=jnp.float32)
            for place in range(2):
                tile = summed[:, place * width : (place + 1) * width]
                own_ref[start + first + place] = tile[:half]
                other_ref[start + first + place] = tile[half:].astype(other_ref.dtype)


def ladder_partials(amps, left, right):
    items, terms, rows, width = amps.shape
    half = left.shape[0] // 2
    return pl.pallas_call(
        ladder_kernel,
        grid=(items // GROUP,),
        in_specs=[
            pl.BlockSpec((GROUP, terms, rows, width), lambda g: (g, 0, 0, 0)),
            pl.BlockSpec(left.shape, lambda g: (0, 0)),
            pl.BlockSpec(right.shape, lambda g: (0, 0, 0)),
        ],
        out_specs=[
            pl.BlockSpec((GROUP, half, width), lambda g: (g, 0, 0)),
            pl.BlockSpec((GROUP, half, width), lambda g: (g, 0, 0)),
        ],
        out_shape=[
            jax.ShapeDtypeStruct((items, half, width), jnp.float32),
            jax.ShapeDtypeStruct((items, half, width), jnp.bfloat16),
        ],
        compiler_params=pltpu.CompilerParams(vmem_limit_bytes=12 << 20),
        cost_estimate=pl.CostEstimate(flops=32 << 27, bytes_accessed=6 << 20, transcendentals=0),
        name="ladder_partials",
    )(amps, left, right)


def sum_kernel(*refs):
    out_ref = refs[-1]
    total = refs[0][...].astype(jnp.float32)
    for part_ref in refs[1:-1]:
        total = total + part_ref[...].astype(jnp.float32)
    out_ref[...] = total.astype(out_ref.dtype)


def sum_parts(parts):
    size = parts[0].size
    return pl.pallas_call(
        sum_kernel,
        in_specs=[pl.BlockSpec(memory_space=pltpu.VMEM)] * len(parts),
        out_specs=pl.BlockSpec(memory_space=pltpu.VMEM),
        out_shape=jax.ShapeDtypeStruct(parts[0].shape, parts[0].dtype),
        cost_estimate=pl.CostEstimate(flops=8 * size, bytes_accessed=18 * size, transcendentals=0),
        name="sum_parts",
    )(*parts)


def shards(
    amplitudes,
    cycle_ints,
    cycle_src,
    cycle_wsel,
    ladder_src,
    owner_order,
    first_integral_blocks,
    right_ints,
):
    held_tiles = amplitudes[0, 0]
    tile_count, row_count, width = held_tiles.shape

    outgoing = gather_tiles(owner_order, ladder_src.T, held_tiles)
    arriving = lax.all_to_all(outgoing, "vir", split_axis=0, concat_axis=0, tiled=True)

    holders = lax.axis_size("occ")
    me = lax.axis_index("occ").astype(jnp.int32).reshape(1)
    partials = cycle_partials(me, holders, cycle_src.T, cycle_wsel.T, held_tiles, cycle_ints[0, 0])
    parts = [partials[0]]
    for step in SENDS:
        ring = [(k, (k + step) % holders) for k in range(holders)]
        parts.append(lax.ppermute(partials[step], "occ", ring))
    arriving, *parts = lax.optimization_barrier((arriving, *parts))
    cycle_part = sum_parts(parts)[None, None]

    replica = lax.axis_index("rep")
    left = lax.dynamic_slice_in_dim(first_integral_blocks[:, 0], replica * row_count, row_count, 3)
    left = jnp.transpose(left, (2, 1, 0, 3)).reshape(width, -1)
    own_rows = lax.dynamic_slice_in_dim(left, replica * row_count, row_count, 0)
    other_rows = lax.dynamic_slice_in_dim(left, (1 - replica) * row_count, row_count, 0)
    left = jnp.concatenate([own_rows, other_rows], axis=0)
    right = jnp.transpose(right_ints[:, 0], (1, 0, 2, 3)).reshape(right_ints.shape[2], -1, width)

    own, other = ladder_partials(arriving, left, right)
    received = lax.ppermute(other, "rep", [(0, 1), (1, 0)])
    ladder_part = (own + received.astype(jnp.float32)).astype(jnp.bfloat16)[:, None, None]
    return (cycle_part, ladder_part)


def solution(mesh):
    in_specs = (
        P("vir", "occ", None, "rep", None),
        P("occ", None, None, None, None),
        P(),
        P(),
        P(),
        P(),
        P(None, "vir", None, None, None),
        P(None, "vir", None, None, None),
    )
    out_specs = (P("vir", None, "occ", "rep", None), P(None, "occ", "vir", "rep", None))
    return jax.shard_map(shards, mesh=mesh, in_specs=in_specs, out_specs=out_specs, check_vma=False)
```

```python
import jax
import jax.numpy as jnp
from jax import lax
from jax.experimental import pallas as pl
from jax.experimental.pallas import tpu as pltpu
from jax.sharding import PartitionSpec as P

GROUP = 16
TOGETHER = 8
SENDS = (4, 3, 5, 2, 6, 1, 7)
SPLITS = 4


def gather_kernel(order_hbm, src_hbm, tiles_hbm, out_hbm, order_ref, src_ref, tiles_ref, out_ref, sems):
    count, terms = out_ref.shape[0], out_ref.shape[1]
    loads = [
        pltpu.make_async_copy(order_hbm, order_ref, sems.at[0]),
        pltpu.make_async_copy(src_hbm, src_ref, sems.at[1]),
        pltpu.make_async_copy(tiles_hbm, tiles_ref, sems.at[2]),
    ]
    for load in loads:
        load.start()
    for load in loads:
        load.wait()

    def one(m, carry):
        slot = order_ref[m]
        for p in range(terms):
            out_ref[m, p] = tiles_ref[src_ref[p, slot]]
        return carry

    share = count // SPLITS
    stores = []
    for part in range(SPLITS):
        lax.fori_loop(part * share, (part + 1) * share, one, 0, unroll=8)
        block = pl.ds(part * share, share)
        stores.append(pltpu.make_async_copy(out_ref.at[block], out_hbm.at[block], sems.at[3 + part]))
        stores[-1].start()
    for store in stores:
        store.wait()


def in_hbm(array):
    return pltpu.with_memory_space_constraint(array, pltpu.HBM)


def whole(shape):
    return pl.BlockSpec(shape, lambda g, *_: (0,) * len(shape))


def gather_tiles(order, src, tiles):
    terms, count = src.shape
    out_shape = (count, terms) + tiles.shape[1:]
    return pl.pallas_call(
        gather_kernel,
        in_specs=[pl.BlockSpec(memory_space=pltpu.HBM)] * 3,
        out_specs=pl.BlockSpec(memory_space=pltpu.HBM),
        out_shape=pltpu.HBM(out_shape, tiles.dtype),
        scratch_shapes=[
            pltpu.SMEM(order.shape, order.dtype),
            pltpu.SMEM(src.shape, src.dtype),
            pltpu.VMEM(tiles.shape, tiles.dtype),
            pltpu.VMEM(out_shape, tiles.dtype),
            pltpu.SemaphoreType.DMA((3 + SPLITS,)),
        ],
        compiler_params=pltpu.CompilerParams(vmem_limit_bytes=8 << 20),
        cost_estimate=pl.CostEstimate(flops=0, bytes_accessed=4 << 20, transcendentals=0),
        name="outgoing_tiles",
    )(in_hbm(order), in_hbm(src), in_hbm(tiles))


def cycle_kernel(me_ref, src_ref, wsel_ref, amps_ref, ints_ref, *refs):
    *out_hbm, out_ref, sems = refs
    terms, holders, share = src_ref.shape[0], out_ref.shape[0], out_ref.shape[1]
    me = me_ref[0]
    stores = []
    for step in SENDS + (0,):
        base = lax.rem(me + step, holders) * share

        def one(t, carry):
            s = base + t
            left = jnp.concatenate([amps_ref[src_ref[p, s]] for p in range(terms)], axis=1)
            right = jnp.concatenate([ints_ref[wsel_ref[p, s]] for p in range(terms)], axis=0)
            total = jnp.dot(left, right, preferred_element_type=jnp.float32)
            out_ref[step, t] = total.astype(out_ref.dtype)
            return carry

        lax.fori_loop(0, share, one, 0, unroll=4)
        stores.append(pltpu.make_async_copy(out_ref.at[step], out_hbm[step], sems.at[step]))
        stores[-1].start()
    for store in stores:
        store.wait()


def cycle_partials(me, holders, src, wsel, amps, ints):
    share = src.shape[1] // holders
    out_shape = (share,) + amps.shape[1:]
    return pl.pallas_call(
        cycle_kernel,
        grid_spec=pltpu.PrefetchScalarGridSpec(
            num_scalar_prefetch=3,
            grid=(1,),
            in_specs=[whole(amps.shape), whole(ints.shape)],
            out_specs=[pl.BlockSpec(memory_space=pltpu.HBM)] * holders,
            scratch_shapes=[
                pltpu.VMEM((holders,) + out_shape, jnp.bfloat16),
                pltpu.SemaphoreType.DMA((holders,)),
            ],
        ),
        out_shape=[pltpu.HBM(out_shape, jnp.bfloat16)] * holders,
        compiler_params=pltpu.CompilerParams(vmem_limit_bytes=12 << 20),
        cost_estimate=pl.CostEstimate(flops=2 * 64 * 64 * 256 * 128, bytes_accessed=4 << 20, transcendentals=0),
        name="cycle_partials",
    )(me, src, wsel, amps, ints)


def ladder_kernel(amps_ref, left_ref, right_ref, own_ref, other_ref):
    group, terms, rows, width = amps_ref.shape
    vectors = right_ref.shape[1] // width
    half = own_ref.shape[1]
    left = left_ref[...]
    sub = min(TOGETHER, group)
    for start in range(0, group, sub):
        halves = []
        for p in range(terms):
            tiles = amps_ref[start : start + sub, p].reshape(sub * rows, width)
            product = lax.dot_general(
                tiles, right_ref[p], (((1,), (1,)), ((), ())), preferred_element_type=jnp.float32
            )
            halves.append(product.astype(jnp.bfloat16))
        for first in range(0, sub, 2):
            columns = []
            for i in (first, first + 1):
                columns.append(
                    jnp.concatenate(
                        [
                            halves[p][i * rows : (i + 1) * rows, q * width : (q + 1) * width]
                            for p in range(terms)
                            for q in range(vectors)
                        ],
                        axis=0,
                    )
                )
            summed = jnp.dot(left, jnp.concatenate(columns, axis=1), preferred_element_type=jnp.float32)
            for place in range(2):
                tile = summed[:, place * width : (place + 1) * width]
                own_ref[start + first + place] = tile[:half]
                other_ref[start + first + place] = tile[half:].astype(other_ref.dtype)


def ladder_partials(amps, left, right):
    items, terms, rows, width = amps.shape
    half = left.shape[0] // 2
    return pl.pallas_call(
        ladder_kernel,
        grid=(items // GROUP,),
        in_specs=[
            pl.BlockSpec((GROUP, terms, rows, width), lambda g: (g, 0, 0, 0)),
            pl.BlockSpec(left.shape, lambda g: (0, 0)),
            pl.BlockSpec(right.shape, lambda g: (0, 0, 0)),
        ],
        out_specs=[
            pl.BlockSpec((GROUP, half, width), lambda g: (g, 0, 0)),
            pl.BlockSpec((GROUP, half, width), lambda g: (g, 0, 0)),
        ],
        out_shape=[
            jax.ShapeDtypeStruct((items, half, width), jnp.float32),
            jax.ShapeDtypeStruct((items, half, width), jnp.bfloat16),
        ],
        compiler_params=pltpu.CompilerParams(vmem_limit_bytes=12 << 20),
        cost_estimate=pl.CostEstimate(flops=32 << 27, bytes_accessed=6 << 20, transcendentals=0),
        name="ladder_partials",
    )(amps, left, right)


def sum_kernel(*refs):
    out_ref = refs[-1]
    total = refs[0][...].astype(jnp.float32)
    for part_ref in refs[1:-1]:
        total = total + part_ref[...].astype(jnp.float32)
    out_ref[...] = total.astype(out_ref.dtype)


def sum_parts(parts):
    size = parts[0].size
    return pl.pallas_call(
        sum_kernel,
        in_specs=[pl.BlockSpec(memory_space=pltpu.VMEM)] * len(parts),
        out_specs=pl.BlockSpec(memory_space=pltpu.VMEM),
        out_shape=jax.ShapeDtypeStruct(parts[0].shape, parts[0].dtype),
        cost_estimate=pl.CostEstimate(flops=8 * size, bytes_accessed=18 * size, transcendentals=0),
        name="sum_parts",
    )(*parts)


def final_kernel(own_ref, received_ref, out_hbm, out_ref, sems):
    items = out_ref.shape[0]
    share = items // SPLITS
    stores = []
    for part in range(SPLITS):
        block = pl.ds(part * share, share)
        total = own_ref[block] + received_ref[block].astype(jnp.float32)
        out_ref[block] = total.astype(out_ref.dtype)
        stores.append(pltpu.make_async_copy(out_ref.at[block], out_hbm.at[block], sems.at[part]))
        stores[-1].start()
    for store in stores:
        store.wait()


def final_sum(own, received):
    vmem = pl.BlockSpec(memory_space=pltpu.VMEM)
    return pl.pallas_call(
        final_kernel,
        in_specs=[vmem, vmem],
        out_specs=pl.BlockSpec(memory_space=pltpu.HBM),
        out_shape=pltpu.HBM(own.shape, received.dtype),
        scratch_shapes=[pltpu.VMEM(own.shape, received.dtype), pltpu.SemaphoreType.DMA((SPLITS,))],
        compiler_params=pltpu.CompilerParams(vmem_limit_bytes=12 << 20),
        cost_estimate=pl.CostEstimate(flops=own.size, bytes_accessed=8 * own.size, transcendentals=0),
        name="final_sum",
    )(own, received)


def shards(
    amplitudes,
    cycle_ints,
    cycle_src,
    cycle_wsel,
    ladder_src,
    owner_order,
    first_integral_blocks,
    right_ints,
):
    held_tiles = amplitudes[0, 0]
    tile_count, row_count, width = held_tiles.shape

    outgoing = gather_tiles(owner_order, ladder_src.T, held_tiles)
    arriving = lax.all_to_all(outgoing, "vir", split_axis=0, concat_axis=0, tiled=True)

    holders = lax.axis_size("occ")
    me = lax.axis_index("occ").astype(jnp.int32).reshape(1)
    partials = cycle_partials(me, holders, cycle_src.T, cycle_wsel.T, held_tiles, cycle_ints[0, 0])
    parts = [partials[0]]
    for step in SENDS:
        ring = [(k, (k + step) % holders) for k in range(holders)]
        parts.append(lax.ppermute(partials[step], "occ", ring))
    arriving, *parts = lax.optimization_barrier((arriving, *parts))
    cycle_part = sum_parts(parts)[None, None]

    replica = lax.axis_index("rep")
    left = lax.dynamic_slice_in_dim(first_integral_blocks[:, 0], replica * row_count, row_count, 3)
    left = jnp.transpose(left, (2, 1, 0, 3)).reshape(width, -1)
    own_rows = lax.dynamic_slice_in_dim(left, replica * row_count, row_count, 0)
    other_rows = lax.dynamic_slice_in_dim(left, (1 - replica) * row_count, row_count, 0)
    left = jnp.concatenate([own_rows, other_rows], axis=0)
    right = jnp.transpose(right_ints[:, 0], (1, 0, 2, 3)).reshape(right_ints.shape[2], -1, width)

    own, other = ladder_partials(arriving, left, right)
    received = lax.ppermute(other, "rep", [(0, 1), (1, 0)])
    ladder_part = final_sum(own, received)[:, None, None]
    return (cycle_part, ladder_part)


def solution(mesh):
    in_specs = (
        P("vir", "occ", None, "rep", None),
        P("occ", None, None, None, None),
        P(),
        P(),
        P(),
        P(),
        P(None, "vir", None, None, None),
        P(None, "vir", None, None, None),
    )
    out_specs = (P("vir", None, "occ", "rep", None), P(None, "occ", "vir", "rep", None))
    return jax.shard_map(shards, mesh=mesh, in_specs=in_specs, out_specs=out_specs, check_vma=False)
```

```python
import jax
import jax.numpy as jnp
from jax import lax
from jax.experimental import pallas as pl
from jax.experimental.pallas import tpu as pltpu
from jax.sharding import PartitionSpec as P

GROUP = 16
TOGETHER = 8
SENDS = (4, 3, 5, 2, 6, 1, 7)
SPLITS = 4


def gather_kernel(order_hbm, src_hbm, tiles_hbm, out_hbm, order_ref, src_ref, tiles_ref, out_ref, sems):
    count, terms = out_ref.shape[0], out_ref.shape[1]
    loads = [
        pltpu.make_async_copy(order_hbm, order_ref, sems.at[0]),
        pltpu.make_async_copy(src_hbm, src_ref, sems.at[1]),
        pltpu.make_async_copy(tiles_hbm, tiles_ref, sems.at[2]),
    ]
    for load in loads:
        load.start()
    for load in loads:
        load.wait()

    def one(m, carry):
        slot = order_ref[m]
        for p in range(terms):
            out_ref[m, p] = tiles_ref[src_ref[p, slot]]
        return carry

    share = count // SPLITS
    stores = []
    for part in range(SPLITS):
        lax.fori_loop(part * share, (part + 1) * share, one, 0, unroll=8)
        block = pl.ds(part * share, share)
        stores.append(pltpu.make_async_copy(out_ref.at[block], out_hbm.at[block], sems.at[3 + part]))
        stores[-1].start()
    for store in stores:
        store.wait()


def in_hbm(array):
    return pltpu.with_memory_space_constraint(array, pltpu.HBM)


def whole(shape):
    return pl.BlockSpec(shape, lambda g, *_: (0,) * len(shape))


def gather_tiles(order, src, tiles):
    terms, count = src.shape
    out_shape = (count, terms) + tiles.shape[1:]
    return pl.pallas_call(
        gather_kernel,
        in_specs=[pl.BlockSpec(memory_space=pltpu.HBM)] * 3,
        out_specs=pl.BlockSpec(memory_space=pltpu.HBM),
        out_shape=pltpu.HBM(out_shape, tiles.dtype),
        scratch_shapes=[
            pltpu.SMEM(order.shape, order.dtype),
            pltpu.SMEM(src.shape, src.dtype),
            pltpu.VMEM(tiles.shape, tiles.dtype),
            pltpu.VMEM(out_shape, tiles.dtype),
            pltpu.SemaphoreType.DMA((3 + SPLITS,)),
        ],
        compiler_params=pltpu.CompilerParams(vmem_limit_bytes=8 << 20),
        cost_estimate=pl.CostEstimate(flops=0, bytes_accessed=4 << 20, transcendentals=0),
        name="outgoing_tiles",
    )(in_hbm(order), in_hbm(src), in_hbm(tiles))


def cycle_kernel(me_ref, src_ref, wsel_ref, amps_ref, ints_ref, *refs):
    *out_hbm, out_ref, sems = refs
    terms, holders, share = src_ref.shape[0], out_ref.shape[0], out_ref.shape[1]
    me = me_ref[0]
    stores = []
    for step in SENDS + (0,):
        base = lax.rem(me + step, holders) * share

        def one(t, carry):
            s = base + t
            left = jnp.concatenate([amps_ref[src_ref[p, s]] for p in range(terms)], axis=1)
            right = jnp.concatenate([ints_ref[wsel_ref[p, s]] for p in range(terms)], axis=0)
            total = jnp.dot(left, right, preferred_element_type=jnp.float32)
            out_ref[step, t] = total.astype(out_ref.dtype)
            return carry

        lax.fori_loop(0, share, one, 0, unroll=4)
        stores.append(pltpu.make_async_copy(out_ref.at[step], out_hbm[step], sems.at[step]))
        stores[-1].start()
    for store in stores:
        store.wait()


def cycle_partials(me, holders, src, wsel, amps, ints):
    share = src.shape[1] // holders
    out_shape = (share,) + amps.shape[1:]
    return pl.pallas_call(
        cycle_kernel,
        grid_spec=pltpu.PrefetchScalarGridSpec(
            num_scalar_prefetch=3,
            grid=(1,),
            in_specs=[whole(amps.shape), whole(ints.shape)],
            out_specs=[pl.BlockSpec(memory_space=pltpu.HBM)] * holders,
            scratch_shapes=[
                pltpu.VMEM((holders,) + out_shape, jnp.bfloat16),
                pltpu.SemaphoreType.DMA((holders,)),
            ],
        ),
        out_shape=[pltpu.HBM(out_shape, jnp.bfloat16)] * holders,
        compiler_params=pltpu.CompilerParams(vmem_limit_bytes=12 << 20),
        cost_estimate=pl.CostEstimate(flops=2 * 64 * 64 * 256 * 128, bytes_accessed=4 << 20, transcendentals=0),
        name="cycle_partials",
    )(me, src, wsel, amps, ints)


def ladder_kernel(amps_ref, left_ref, right_ref, own_ref, other_ref):
    group, terms, rows, width = amps_ref.shape
    vectors = right_ref.shape[1] // width
    half = own_ref.shape[1]
    left = left_ref[...]
    sub = min(TOGETHER, group)
    for start in range(0, group, sub):
        halves = []
        for p in range(terms):
            tiles = amps_ref[start : start + sub, p].reshape(sub * rows, width)
            product = lax.dot_general(
                tiles, right_ref[p], (((1,), (1,)), ((), ())), preferred_element_type=jnp.float32
            )
            halves.append(product.astype(jnp.bfloat16))
        for first in range(0, sub, 2):
            columns = []
            for i in (first, first + 1):
                columns.append(
                    jnp.concatenate(
                        [
                            halves[p][i * rows : (i + 1) * rows, q * width : (q + 1) * width]
                            for p in range(terms)
                            for q in range(vectors)
                        ],
                        axis=0,
                    )
                )
            summed = jnp.dot(left, jnp.concatenate(columns, axis=1), preferred_element_type=jnp.float32)
            for place in range(2):
                tile = summed[:, place * width : (place + 1) * width]
                own_ref[start + first + place] = tile[:half].astype(own_ref.dtype)
                other_ref[start + first + place] = tile[half:].astype(other_ref.dtype)


def ladder_partials(amps, left, right):
    items, terms, rows, width = amps.shape
    half = left.shape[0] // 2
    return pl.pallas_call(
        ladder_kernel,
        grid=(items // GROUP,),
        in_specs=[
            pl.BlockSpec((GROUP, terms, rows, width), lambda g: (g, 0, 0, 0)),
            pl.BlockSpec(left.shape, lambda g: (0, 0)),
            pl.BlockSpec(right.shape, lambda g: (0, 0, 0)),
        ],
        out_specs=[
            pl.BlockSpec((GROUP, half, width), lambda g: (g, 0, 0)),
            pl.BlockSpec((GROUP, half, width), lambda g: (g, 0, 0)),
        ],
        out_shape=[
            jax.ShapeDtypeStruct((items, half, width), jnp.bfloat16),
            jax.ShapeDtypeStruct((items, half, width), jnp.bfloat16),
        ],
        compiler_params=pltpu.CompilerParams(vmem_limit_bytes=12 << 20),
        cost_estimate=pl.CostEstimate(flops=32 << 27, bytes_accessed=6 << 20, transcendentals=0),
        name="ladder_partials",
    )(amps, left, right)


def sum_kernel(*refs):
    out_ref = refs[-1]
    total = refs[0][...].astype(jnp.float32)
    for part_ref in refs[1:-1]:
        total = total + part_ref[...].astype(jnp.float32)
    out_ref[...] = total.astype(out_ref.dtype)


def sum_parts(parts):
    size = parts[0].size
    return pl.pallas_call(
        sum_kernel,
        in_specs=[pl.BlockSpec(memory_space=pltpu.VMEM)] * len(parts),
        out_specs=pl.BlockSpec(memory_space=pltpu.VMEM),
        out_shape=jax.ShapeDtypeStruct(parts[0].shape, parts[0].dtype),
        cost_estimate=pl.CostEstimate(flops=8 * size, bytes_accessed=18 * size, transcendentals=0),
        name="sum_parts",
    )(*parts)


def final_kernel(own_ref, received_ref, out_hbm, out_ref, sems):
    items = out_ref.shape[0]
    share = items // SPLITS
    stores = []
    for part in range(SPLITS):
        block = pl.ds(part * share, share)
        total = own_ref[block].astype(jnp.float32) + received_ref[block].astype(jnp.float32)
        out_ref[block] = total.astype(out_ref.dtype)
        stores.append(pltpu.make_async_copy(out_ref.at[block], out_hbm.at[block], sems.at[part]))
        stores[-1].start()
    for store in stores:
        store.wait()


def final_sum(own, received):
    vmem = pl.BlockSpec(memory_space=pltpu.VMEM)
    return pl.pallas_call(
        final_kernel,
        in_specs=[vmem, vmem],
        out_specs=pl.BlockSpec(memory_space=pltpu.HBM),
        out_shape=pltpu.HBM(own.shape, received.dtype),
        scratch_shapes=[pltpu.VMEM(own.shape, received.dtype), pltpu.SemaphoreType.DMA((SPLITS,))],
        compiler_params=pltpu.CompilerParams(vmem_limit_bytes=12 << 20),
        cost_estimate=pl.CostEstimate(flops=own.size, bytes_accessed=8 * own.size, transcendentals=0),
        name="final_sum",
    )(own, received)


def shards(
    amplitudes,
    cycle_ints,
    cycle_src,
    cycle_wsel,
    ladder_src,
    owner_order,
    first_integral_blocks,
    right_ints,
):
    held_tiles = amplitudes[0, 0]
    tile_count, row_count, width = held_tiles.shape

    outgoing = gather_tiles(owner_order, ladder_src.T, held_tiles)
    arriving = lax.all_to_all(outgoing, "vir", split_axis=0, concat_axis=0, tiled=True)

    holders = lax.axis_size("occ")
    me = lax.axis_index("occ").astype(jnp.int32).reshape(1)
    partials = cycle_partials(me, holders, cycle_src.T, cycle_wsel.T, held_tiles, cycle_ints[0, 0])
    parts = [partials[0]]
    for step in SENDS:
        ring = [(k, (k + step) % holders) for k in range(holders)]
        parts.append(lax.ppermute(partials[step], "occ", ring))
    arriving, *parts = lax.optimization_barrier((arriving, *parts))
    cycle_part = sum_parts(parts)[None, None]

    replica = lax.axis_index("rep")
    left = lax.dynamic_slice_in_dim(first_integral_blocks[:, 0], replica * row_count, row_count, 3)
    left = jnp.transpose(left, (2, 1, 0, 3)).reshape(width, -1)
    own_rows = lax.dynamic_slice_in_dim(left, replica * row_count, row_count, 0)
    other_rows = lax.dynamic_slice_in_dim(left, (1 - replica) * row_count, row_count, 0)
    left = jnp.concatenate([own_rows, other_rows], axis=0)
    right = jnp.transpose(right_ints[:, 0], (1, 0, 2, 3)).reshape(right_ints.shape[2], -1, width)

    own, other = ladder_partials(arriving, left, right)
    received = lax.ppermute(other, "rep", [(0, 1), (1, 0)])
    ladder_part = final_sum(own, received)[:, None, None]
    return (cycle_part, ladder_part)


def solution(mesh):
    in_specs = (
        P("vir", "occ", None, "rep", None),
        P("occ", None, None, None, None),
        P(),
        P(),
        P(),
        P(),
        P(None, "vir", None, None, None),
        P(None, "vir", None, None, None),
    )
    out_specs = (P("vir", None, "occ", "rep", None), P(None, "occ", "vir", "rep", None))
    return jax.shard_map(shards, mesh=mesh, in_specs=in_specs, out_specs=out_specs, check_vma=False)
```

```python
import functools

import jax
import jax.numpy as jnp
from jax import lax
from jax.experimental import pallas as pl
from jax.experimental.pallas import tpu as pltpu
from jax.sharding import PartitionSpec as P

GROUP = 16
TOGETHER = 8
SENDS = (4, 3, 5, 2, 6, 1, 7)
SPLITS = 4


def gather_kernel(order_hbm, src_hbm, tiles_hbm, out_hbm, order_ref, src_ref, tiles_ref, out_ref, sems):
    count, terms = out_ref.shape[0], out_ref.shape[1]
    loads = [
        pltpu.make_async_copy(order_hbm, order_ref, sems.at[0]),
        pltpu.make_async_copy(src_hbm, src_ref, sems.at[1]),
        pltpu.make_async_copy(tiles_hbm, tiles_ref, sems.at[2]),
    ]
    for load in loads:
        load.start()
    for load in loads:
        load.wait()

    def one(m, carry):
        slot = order_ref[m]
        for p in range(terms):
            out_ref[m, p] = tiles_ref[src_ref[p, slot]]
        return carry

    share = count // SPLITS
    stores = []
    for part in range(SPLITS):
        lax.fori_loop(part * share, (part + 1) * share, one, 0, unroll=8)
        block = pl.ds(part * share, share)
        stores.append(pltpu.make_async_copy(out_ref.at[block], out_hbm.at[block], sems.at[3 + part]))
        stores[-1].start()
    for store in stores:
        store.wait()


def in_hbm(array):
    return pltpu.with_memory_space_constraint(array, pltpu.HBM)


def whole(shape):
    return pl.BlockSpec(shape, lambda g, *_: (0,) * len(shape))


def gather_tiles(order, src, tiles):
    terms, count = src.shape
    out_shape = (count, terms) + tiles.shape[1:]
    return pl.pallas_call(
        gather_kernel,
        in_specs=[pl.BlockSpec(memory_space=pltpu.HBM)] * 3,
        out_specs=pl.BlockSpec(memory_space=pltpu.HBM),
        out_shape=pltpu.HBM(out_shape, tiles.dtype),
        scratch_shapes=[
            pltpu.SMEM(order.shape, order.dtype),
            pltpu.SMEM(src.shape, src.dtype),
            pltpu.VMEM(tiles.shape, tiles.dtype),
            pltpu.VMEM(out_shape, tiles.dtype),
            pltpu.SemaphoreType.DMA((3 + SPLITS,)),
        ],
        compiler_params=pltpu.CompilerParams(vmem_limit_bytes=8 << 20),
        cost_estimate=pl.CostEstimate(flops=0, bytes_accessed=4 << 20, transcendentals=0),
        name="outgoing_tiles",
    )(in_hbm(order), in_hbm(src), in_hbm(tiles))


def cycle_kernel(me_ref, src_ref, wsel_ref, amps_ref, ints_ref, *refs):
    *out_hbm, out_ref, sems = refs
    terms, holders, share = src_ref.shape[0], out_ref.shape[0], out_ref.shape[1]
    me = me_ref[0]
    stores = []
    for step in SENDS + (0,):
        base = lax.rem(me + step, holders) * share

        def one(t, carry):
            s = base + t
            left = jnp.concatenate([amps_ref[src_ref[p, s]] for p in range(terms)], axis=1)
            right = jnp.concatenate([ints_ref[wsel_ref[p, s]] for p in range(terms)], axis=0)
            total = jnp.dot(left, right, preferred_element_type=jnp.float32)
            out_ref[step, t] = total.astype(out_ref.dtype)
            return carry

        lax.fori_loop(0, share, one, 0, unroll=4)
        stores.append(pltpu.make_async_copy(out_ref.at[step], out_hbm[step], sems.at[step]))
        stores[-1].start()
    for store in stores:
        store.wait()


def cycle_partials(me, holders, src, wsel, amps, ints):
    share = src.shape[1] // holders
    out_shape = (share,) + amps.shape[1:]
    return pl.pallas_call(
        cycle_kernel,
        grid_spec=pltpu.PrefetchScalarGridSpec(
            num_scalar_prefetch=3,
            grid=(1,),
            in_specs=[whole(amps.shape), whole(ints.shape)],
            out_specs=[pl.BlockSpec(memory_space=pltpu.HBM)] * holders,
            scratch_shapes=[
                pltpu.VMEM((holders,) + out_shape, jnp.bfloat16),
                pltpu.SemaphoreType.DMA((holders,)),
            ],
        ),
        out_shape=[pltpu.HBM(out_shape, jnp.bfloat16)] * holders,
        compiler_params=pltpu.CompilerParams(vmem_limit_bytes=12 << 20),
        cost_estimate=pl.CostEstimate(flops=2 * 64 * 64 * 256 * 128, bytes_accessed=4 << 20, transcendentals=0),
        name="cycle_partials",
    )(me, src, wsel, amps, ints)


def ladder_kernel(amps_ref, left_ref, right_ref, own_ref, early_ref, late_ref, other_ref):
    group, terms, rows, width = amps_ref.shape
    vectors = right_ref.shape[1] // width
    half = own_ref.shape[1]
    left = left_ref[...]
    sub = min(TOGETHER, group)
    for start in range(0, group, sub):
        halves = []
        for p in range(terms):
            tiles = amps_ref[start : start + sub, p].reshape(sub * rows, width)
            product = lax.dot_general(
                tiles, right_ref[p], (((1,), (1,)), ((), ())), preferred_element_type=jnp.float32
            )
            halves.append(product.astype(jnp.bfloat16))
        for first in range(0, sub, 2):
            columns = []
            for i in (first, first + 1):
                columns.append(
                    jnp.concatenate(
                        [
                            halves[p][i * rows : (i + 1) * rows, q * width : (q + 1) * width]
                            for p in range(terms)
                            for q in range(vectors)
                        ],
                        axis=0,
                    )
                )
            summed = jnp.dot(left, jnp.concatenate(columns, axis=1), preferred_element_type=jnp.float32)
            for place in range(2):
                tile = summed[:, place * width : (place + 1) * width]
                own_ref[start + first + place] = tile[:half].astype(own_ref.dtype)
                other_ref[start + first + place] = tile[half:].astype(other_ref.dtype)
    last = pl.num_programs(0) - 1

    @pl.when(pl.program_id(0) < last)
    def _():
        early_ref[...] = other_ref[...]

    @pl.when(pl.program_id(0) == last)
    def _():
        late_ref[...] = other_ref[...]


def ladder_partials(amps, left, right):
    items, terms, rows, width = amps.shape
    half = left.shape[0] // 2
    return pl.pallas_call(
        ladder_kernel,
        grid=(items // GROUP,),
        in_specs=[
            pl.BlockSpec((GROUP, terms, rows, width), lambda g: (g, 0, 0, 0)),
            pl.BlockSpec(left.shape, lambda g: (0, 0)),
            pl.BlockSpec(right.shape, lambda g: (0, 0, 0)),
        ],
        out_specs=[
            pl.BlockSpec((GROUP, half, width), lambda g: (g, 0, 0)),
            pl.BlockSpec((GROUP, half, width), lambda g: (jnp.minimum(g, items // GROUP - 2), 0, 0)),
            pl.BlockSpec((GROUP, half, width), lambda g: (0, 0, 0)),
        ],
        out_shape=[
            jax.ShapeDtypeStruct((items, half, width), jnp.bfloat16),
            jax.ShapeDtypeStruct((items - GROUP, half, width), jnp.bfloat16),
            jax.ShapeDtypeStruct((GROUP, half, width), jnp.bfloat16),
        ],
        scratch_shapes=[pltpu.VMEM((GROUP, half, width), jnp.bfloat16)],
        compiler_params=pltpu.CompilerParams(vmem_limit_bytes=12 << 20),
        cost_estimate=pl.CostEstimate(flops=32 << 27, bytes_accessed=6 << 20, transcendentals=0),
        name="ladder_partials",
    )(amps, left, right)


def sum_kernel(*refs):
    out_ref = refs[-1]
    total = refs[0][...].astype(jnp.float32)
    for part_ref in refs[1:-1]:
        total = total + part_ref[...].astype(jnp.float32)
    out_ref[...] = total.astype(out_ref.dtype)


def sum_parts(parts):
    size = parts[0].size
    return pl.pallas_call(
        sum_kernel,
        in_specs=[pl.BlockSpec(memory_space=pltpu.VMEM)] * len(parts),
        out_specs=pl.BlockSpec(memory_space=pltpu.VMEM),
        out_shape=jax.ShapeDtypeStruct(parts[0].shape, parts[0].dtype),
        cost_estimate=pl.CostEstimate(flops=8 * size, bytes_accessed=18 * size, transcendentals=0),
        name="sum_parts",
    )(*parts)


def final_kernel(first, pieces, own_ref, received_ref, *refs):
    out_hbm, out_ref, sems = refs[-3:]
    share = received_ref.shape[0] // pieces
    stores = []
    for part in range(pieces):
        block = pl.ds(part * share, share)
        place = pl.ds(first + part * share, share)
        total = own_ref[place].astype(jnp.float32) + received_ref[block].astype(jnp.float32)
        out_ref[block] = total.astype(out_ref.dtype)
        stores.append(pltpu.make_async_copy(out_ref.at[block], out_hbm.at[place], sems.at[part]))
        stores[-1].start()
    for store in stores:
        store.wait()


def final_sum(first, pieces, own, received, *earlier):
    vmem, hbm = pl.BlockSpec(memory_space=pltpu.VMEM), pl.BlockSpec(memory_space=pltpu.HBM)
    return pl.pallas_call(
        functools.partial(final_kernel, first, pieces),
        in_specs=[vmem, vmem] + [hbm] * len(earlier),
        out_specs=hbm,
        out_shape=pltpu.HBM(own.shape, received.dtype),
        scratch_shapes=[pltpu.VMEM(received.shape, received.dtype), pltpu.SemaphoreType.DMA((pieces,))],
        input_output_aliases={2: 0} if earlier else {},
        compiler_params=pltpu.CompilerParams(vmem_limit_bytes=8 << 20),
        cost_estimate=pl.CostEstimate(flops=received.size, bytes_accessed=6 * received.size, transcendentals=0),
        name="final_sum",
    )(own, received, *earlier)


def shards(
    amplitudes,
    cycle_ints,
    cycle_src,
    cycle_wsel,
    ladder_src,
    owner_order,
    first_integral_blocks,
    right_ints,
):
    held_tiles = amplitudes[0, 0]
    tile_count, row_count, width = held_tiles.shape

    outgoing = gather_tiles(owner_order, ladder_src.T, held_tiles)
    arriving = lax.all_to_all(outgoing, "vir", split_axis=0, concat_axis=0, tiled=True)

    holders = lax.axis_size("occ")
    me = lax.axis_index("occ").astype(jnp.int32).reshape(1)
    partials = cycle_partials(me, holders, cycle_src.T, cycle_wsel.T, held_tiles, cycle_ints[0, 0])
    parts = [partials[0]]
    for step in SENDS:
        ring = [(k, (k + step) % holders) for k in range(holders)]
        parts.append(lax.ppermute(partials[step], "occ", ring))
    cycle_part = sum_parts(parts)
    arriving, cycle_part = lax.optimization_barrier((arriving, cycle_part))
    cycle_part = cycle_part[None, None]

    replica = lax.axis_index("rep")
    left = lax.dynamic_slice_in_dim(first_integral_blocks[:, 0], replica * row_count, row_count, 3)
    left = jnp.transpose(left, (2, 1, 0, 3)).reshape(width, -1)
    own_rows = lax.dynamic_slice_in_dim(left, replica * row_count, row_count, 0)
    other_rows = lax.dynamic_slice_in_dim(left, (1 - replica) * row_count, row_count, 0)
    left = jnp.concatenate([own_rows, other_rows], axis=0)
    right = jnp.transpose(right_ints[:, 0], (1, 0, 2, 3)).reshape(right_ints.shape[2], -1, width)

    own, early, late = ladder_partials(arriving, left, right)
    swap = [(0, 1), (1, 0)]
    early = lax.ppermute(early, "rep", swap)
    late = lax.ppermute(late, "rep", swap)
    ladder_part = final_sum(0, 3, own, early)
    ladder_part = final_sum(early.shape[0], 2, own, late, ladder_part)[:, None, None]
    return (cycle_part, ladder_part)


def solution(mesh):
    in_specs = (
        P("vir", "occ", None, "rep", None),
        P("occ", None, None, None, None),
        P(),
        P(),
        P(),
        P(),
        P(None, "vir", None, None, None),
        P(None, "vir", None, None, None),
    )
    out_specs = (P("vir", None, "occ", "rep", None), P(None, "occ", "vir", "rep", None))
    return jax.shard_map(shards, mesh=mesh, in_specs=in_specs, out_specs=out_specs, check_vma=False)
```

```python
import jax
import jax.numpy as jnp
from jax import lax
from jax.experimental import pallas as pl
from jax.experimental.pallas import tpu as pltpu
from jax.sharding import PartitionSpec as P

GROUP = 32
TOGETHER = 8
SENDS = (4, 3, 5, 2, 6, 1, 7)
SPLITS = 4


def gather_kernel(order_hbm, src_hbm, tiles_hbm, out_hbm, order_ref, src_ref, tiles_ref, out_ref, sems):
    count, terms = out_ref.shape[0], out_ref.shape[1]
    loads = [
        pltpu.make_async_copy(order_hbm, order_ref, sems.at[0]),
        pltpu.make_async_copy(src_hbm, src_ref, sems.at[1]),
        pltpu.make_async_copy(tiles_hbm, tiles_ref, sems.at[2]),
    ]
    for load in loads:
        load.start()
    for load in loads:
        load.wait()

    def one(m, carry):
        slot = order_ref[m]
        for p in range(terms):
            out_ref[m, p] = tiles_ref[src_ref[p, slot]]
        return carry

    share = count // SPLITS
    stores = []
    for part in range(SPLITS):
        lax.fori_loop(part * share, (part + 1) * share, one, 0, unroll=8)
        block = pl.ds(part * share, share)
        stores.append(pltpu.make_async_copy(out_ref.at[block], out_hbm.at[block], sems.at[3 + part]))
        stores[-1].start()
    for store in stores:
        store.wait()


def in_hbm(array):
    return pltpu.with_memory_space_constraint(array, pltpu.HBM)


def whole(shape):
    return pl.BlockSpec(shape, lambda g, *_: (0,) * len(shape))


def gather_tiles(order, src, tiles):
    terms, count = src.shape
    out_shape = (count, terms) + tiles.shape[1:]
    return pl.pallas_call(
        gather_kernel,
        in_specs=[pl.BlockSpec(memory_space=pltpu.HBM)] * 3,
        out_specs=pl.BlockSpec(memory_space=pltpu.HBM),
        out_shape=pltpu.HBM(out_shape, tiles.dtype),
        scratch_shapes=[
            pltpu.SMEM(order.shape, order.dtype),
            pltpu.SMEM(src.shape, src.dtype),
            pltpu.VMEM(tiles.shape, tiles.dtype),
            pltpu.VMEM(out_shape, tiles.dtype),
            pltpu.SemaphoreType.DMA((3 + SPLITS,)),
        ],
        compiler_params=pltpu.CompilerParams(vmem_limit_bytes=8 << 20),
        cost_estimate=pl.CostEstimate(flops=0, bytes_accessed=4 << 20, transcendentals=0),
        name="outgoing_tiles",
    )(in_hbm(order), in_hbm(src), in_hbm(tiles))


def cycle_kernel(me_ref, src_ref, wsel_ref, amps_ref, ints_ref, *refs):
    *out_hbm, out_ref, sems = refs
    terms, holders, share = src_ref.shape[0], out_ref.shape[0], out_ref.shape[1]
    me = me_ref[0]
    stores = []
    for step in SENDS + (0,):
        base = lax.rem(me + step, holders) * share

        def one(t, carry):
            s = base + t
            left = jnp.concatenate([amps_ref[src_ref[p, s]] for p in range(terms)], axis=1)
            right = jnp.concatenate([ints_ref[wsel_ref[p, s]] for p in range(terms)], axis=0)
            total = jnp.dot(left, right, preferred_element_type=jnp.float32)
            out_ref[step, t] = total.astype(out_ref.dtype)
            return carry

        lax.fori_loop(0, share, one, 0, unroll=4)
        stores.append(pltpu.make_async_copy(out_ref.at[step], out_hbm[step], sems.at[step]))
        stores[-1].start()
    for store in stores:
        store.wait()


def cycle_partials(me, holders, src, wsel, amps, ints):
    share = src.shape[1] // holders
    out_shape = (share,) + amps.shape[1:]
    return pl.pallas_call(
        cycle_kernel,
        grid_spec=pltpu.PrefetchScalarGridSpec(
            num_scalar_prefetch=3,
            grid=(1,),
            in_specs=[whole(amps.shape), whole(ints.shape)],
            out_specs=[pl.BlockSpec(memory_space=pltpu.HBM)] * holders,
            scratch_shapes=[
                pltpu.VMEM((holders,) + out_shape, jnp.bfloat16),
                pltpu.SemaphoreType.DMA((holders,)),
            ],
        ),
        out_shape=[pltpu.HBM(out_shape, jnp.bfloat16)] * holders,
        compiler_params=pltpu.CompilerParams(vmem_limit_bytes=12 << 20),
        cost_estimate=pl.CostEstimate(flops=2 * 64 * 64 * 256 * 128, bytes_accessed=4 << 20, transcendentals=0),
        name="cycle_partials",
    )(me, src, wsel, amps, ints)


def ladder_kernel(amps_ref, left_ref, right_ref, own_ref, other_ref):
    group, terms, rows, width = amps_ref.shape
    vectors = right_ref.shape[1] // width
    half = own_ref.shape[1]
    left = left_ref[...]
    sub = min(TOGETHER, group)
    for start in range(0, group, sub):
        halves = []
        for p in range(terms):
            tiles = amps_ref[start : start + sub, p].reshape(sub * rows, width)
            product = lax.dot_general(
                tiles, right_ref[p], (((1,), (1,)), ((), ())), preferred_element_type=jnp.float32
            )
            halves.append(product.astype(jnp.bfloat16))
        for first in range(0, sub, 2):
            columns = []
            for i in (first, first + 1):
                columns.append(
                    jnp.concatenate(
                        [
                            halves[p][i * rows : (i + 1) * rows, q * width : (q + 1) * width]
                            for p in range(terms)
                            for q in range(vectors)
                        ],
                        axis=0,
                    )
                )
            summed = jnp.dot(left, jnp.concatenate(columns, axis=1), preferred_element_type=jnp.float32)
            for place in range(2):
                tile = summed[:, place * width : (place + 1) * width]
                own_ref[start + first + place] = tile[:half].astype(own_ref.dtype)
                other_ref[start + first + place] = tile[half:].astype(other_ref.dtype)


def ladder_partials(amps, left, right):
    items, terms, rows, width = amps.shape
    half = left.shape[0] // 2
    return pl.pallas_call(
        ladder_kernel,
        grid=(items // GROUP,),
        in_specs=[
            pl.BlockSpec((GROUP, terms, rows, width), lambda g: (g, 0, 0, 0)),
            pl.BlockSpec(left.shape, lambda g: (0, 0)),
            pl.BlockSpec(right.shape, lambda g: (0, 0, 0)),
        ],
        out_specs=[
            pl.BlockSpec((GROUP, half, width), lambda g: (g, 0, 0)),
            pl.BlockSpec((GROUP, half, width), lambda g: (g, 0, 0)),
        ],
        out_shape=[
            jax.ShapeDtypeStruct((items, half, width), jnp.bfloat16),
            jax.ShapeDtypeStruct((items, half, width), jnp.bfloat16),
        ],
        compiler_params=pltpu.CompilerParams(vmem_limit_bytes=12 << 20),
        cost_estimate=pl.CostEstimate(flops=32 << 27, bytes_accessed=6 << 20, transcendentals=0),
        name="ladder_partials",
    )(amps, left, right)


def sum_kernel(*refs):
    out_ref = refs[-1]
    total = refs[0][...].astype(jnp.float32)
    for part_ref in refs[1:-1]:
        total = total + part_ref[...].astype(jnp.float32)
    out_ref[...] = total.astype(out_ref.dtype)


def sum_parts(parts):
    size = parts[0].size
    return pl.pallas_call(
        sum_kernel,
        in_specs=[pl.BlockSpec(memory_space=pltpu.VMEM)] * len(parts),
        out_specs=pl.BlockSpec(memory_space=pltpu.VMEM),
        out_shape=jax.ShapeDtypeStruct(parts[0].shape, parts[0].dtype),
        cost_estimate=pl.CostEstimate(flops=8 * size, bytes_accessed=18 * size, transcendentals=0),
        name="sum_parts",
    )(*parts)


def final_kernel(own_ref, received_ref, out_hbm, out_ref, sems):
    items = out_ref.shape[0]
    share = items // SPLITS
    stores = []
    for part in range(SPLITS):
        block = pl.ds(part * share, share)
        total = own_ref[block].astype(jnp.float32) + received_ref[block].astype(jnp.float32)
        out_ref[block] = total.astype(out_ref.dtype)
        stores.append(pltpu.make_async_copy(out_ref.at[block], out_hbm.at[block], sems.at[part]))
        stores[-1].start()
    for store in stores:
        store.wait()


def final_sum(own, received):
    vmem = pl.BlockSpec(memory_space=pltpu.VMEM)
    return pl.pallas_call(
        final_kernel,
        in_specs=[vmem, vmem],
        out_specs=pl.BlockSpec(memory_space=pltpu.HBM),
        out_shape=pltpu.HBM(own.shape, received.dtype),
        scratch_shapes=[pltpu.VMEM(own.shape, received.dtype), pltpu.SemaphoreType.DMA((SPLITS,))],
        compiler_params=pltpu.CompilerParams(vmem_limit_bytes=12 << 20),
        cost_estimate=pl.CostEstimate(flops=own.size, bytes_accessed=8 * own.size, transcendentals=0),
        name="final_sum",
    )(own, received)


def shards(
    amplitudes,
    cycle_ints,
    cycle_src,
    cycle_wsel,
    ladder_src,
    owner_order,
    first_integral_blocks,
    right_ints,
):
    held_tiles = amplitudes[0, 0]
    tile_count, row_count, width = held_tiles.shape

    outgoing = gather_tiles(owner_order, ladder_src.T, held_tiles)
    arriving = lax.all_to_all(outgoing, "vir", split_axis=0, concat_axis=0, tiled=True)

    holders = lax.axis_size("occ")
    me = lax.axis_index("occ").astype(jnp.int32).reshape(1)
    partials = cycle_partials(me, holders, cycle_src.T, cycle_wsel.T, held_tiles, cycle_ints[0, 0])
    parts = [partials[0]]
    for step in SENDS:
        ring = [(k, (k + step) % holders) for k in range(holders)]
        parts.append(lax.ppermute(partials[step], "occ", ring))
    arriving, *parts = lax.optimization_barrier((arriving, *parts))
    cycle_part = sum_parts(parts)[None, None]

    replica = lax.axis_index("rep")
    left = lax.dynamic_slice_in_dim(first_integral_blocks[:, 0], replica * row_count, row_count, 3)
    left = jnp.transpose(left, (2, 1, 0, 3)).reshape(width, -1)
    own_rows = lax.dynamic_slice_in_dim(left, replica * row_count, row_count, 0)
    other_rows = lax.dynamic_slice_in_dim(left, (1 - replica) * row_count, row_count, 0)
    left = jnp.concatenate([own_rows, other_rows], axis=0)
    right = jnp.transpose(right_ints[:, 0], (1, 0, 2, 3)).reshape(right_ints.shape[2], -1, width)

    own, other = ladder_partials(arriving, left, right)
    received = lax.ppermute(other, "rep", [(0, 1), (1, 0)])
    ladder_part = final_sum(own, received)[:, None, None]
    return (cycle_part, ladder_part)


def solution(mesh):
    in_specs = (
        P("vir", "occ", None, "rep", None),
        P("occ", None, None, None, None),
        P(),
        P(),
        P(),
        P(),
        P(None, "vir", None, None, None),
        P(None, "vir", None, None, None),
    )
    out_specs = (P("vir", None, "occ", "rep", None), P(None, "occ", "vir", "rep", None))
    return jax.shard_map(shards, mesh=mesh, in_specs=in_specs, out_specs=out_specs, check_vma=False)
```
